128 devices in a mesh: grp: 4 (over x), mem: 32 (over z, y, core).
Axes of the slice: x: 4, y: 4, z: 4, core: 2. Of those that a mesh axis runs over, the one named last changes fastest.
Arguments:
- user_rows: bfloat16 [16384, 2048], P(('grp', 'mem')), may hold values from -6 to 6
- projection: bfloat16 [2048, 2048], replicated, may hold values from -0.125 to 0.125
- item_table: bfloat16 [8192, 2048], P(('grp', 'mem')), may hold values from -8 to 8
- positive: int32 [16384], P(('grp', 'mem')), may hold values from 0 to 8191, as said below
- negatives: int32 [4, 1024], P(None, ('grp', 'mem')), may hold values from 0 to 8191, as said below
Outputs:
- user_grad: bfloat16 [16384, 2048], P(('grp', 'mem'))
- item_grad: float32 [8192, 2048], P(('grp', 'mem'))
The draws below stay inside these ranges and needn't reach their ends.
Inputs may be any that keep to these rules, and one draw needn't show every extreme that they name: `positive`: owner o (grp-major order over grp and mem) holds item rows o * 64 to (o + 1) * 64 - 1. Among the 128 rows of any one device, at most 4 positives lie with any one owner, and one owner receives exactly 4 from every device. `negatives`: in every group, negative j is one of the item rows of owner j // 8.
All inputs are finite; a program needn't handle non-finite values.
Results may differ from the reference program's by a relative error of at most 0.0075.
Values may be sent and summed in bfloat16 or wider, within the bound.
A program may use at most 64 MiB of HBM per device.

```python
import math
import jax
import jax.numpy as jnp
from jax import lax

D = 2048
U_DEV = 128
ITEMS = 8192
NEG = 1024
USERS = 16384
N_GRP = 4
N_MEM = 32


def draw_item_table(key, part):
    key_base = jax.random.fold_in(key, 0)
    base_rows = jax.random.truncated_normal(key_base, -4.0, 4.0, (ITEMS, D), jnp.float32)
    return base_rows.astype(jnp.bfloat16)


def draw_positive(key, part):
    owners = N_GRP * N_MEM
    capacity = 4 * U_DEV // owners
    own_rows = ITEMS // owners
    key_hot, key_start, key_order, key_offset = jax.random.split(key, 4)
    hot_owner = jax.random.randint(key_hot, (), 0, owners)
    starts = jax.random.randint(key_start, (owners, 1), 0, owners - 1)
    step_index = jnp.arange(U_DEV, dtype=jnp.int32)[None, :]
    other_owner = (starts + step_index - capacity) % (owners - 1)
    other_owner = other_owner + (other_owner >= hot_owner).astype(jnp.int32)
    owner_index = jnp.where(step_index < capacity, hot_owner, other_owner)
    scores = jax.random.randint(key_order, (owners, U_DEV), 0, 1 << 20) * U_DEV + step_index
    row_order = jnp.argsort(scores, axis=1, stable=True)
    owner_index = jnp.take_along_axis(owner_index, row_order, axis=1)
    offsets = jax.random.randint(key_offset, (owners, U_DEV), 0, own_rows)
    return (owner_index * own_rows + offsets).reshape(-1).astype(jnp.int32)


def draw_negatives(key, part):
    owners = N_GRP * N_MEM
    own_rows = ITEMS // owners
    column = jnp.arange(NEG, dtype=jnp.int32)[None, :]
    offsets = jax.random.randint(key, (N_GRP, NEG), 0, own_rows)
    return (column // (NEG // owners) * own_rows + offsets).astype(jnp.int32)


def level_of(key, shape, cuts, low, high):
    def one(dim, blocks):
        draws = jax.random.uniform(jax.random.fold_in(jax.random.fold_in(key, 6), dim), (blocks,), jnp.float32, low / len(cuts), high / len(cuts))
        return jnp.repeat(jnp.exp(draws), shape[dim] // blocks).reshape((-1,) + (1,) * (len(shape) - dim - 1))

    gain = one(*cuts[0])
    for cut in cuts[1:]:
        gain = gain * one(*cut)
    return gain


def centred(key, extent, spread, limit, shards=(), kind=jnp.bfloat16):
    gain = level_of(key, extent, shards, -0.22, 0.18) if shards else 1.0
    values = jax.random.normal(key, extent, jnp.float32) * spread * gain
    return jnp.minimum(jnp.maximum(values, -limit), limit).astype(kind)


def setup_inputs(seed: int = 0) -> dict:
    seeds = jax.random.split(jax.random.key(seed), 6)
    user_rows = centred(seeds[0], (USERS, D), 1.0, 6.0, ((0, 128),))
    projection = centred(seeds[1], (D, D), D ** -0.5, 0.125)
    item_table = draw_item_table(jax.random.fold_in(seeds[5], 71), 0)
    positive = draw_positive(jax.random.fold_in(seeds[5], 71), 0)
    negatives = draw_negatives(jax.random.fold_in(seeds[5], 71), 0)
    return {"user_rows": user_rows, "projection": projection, "item_table": item_table, "positive": positive, "negatives": negatives}


def silu_slope(hidden):
    sigmoid_value = jax.nn.sigmoid(hidden)
    return sigmoid_value * (1.0 + hidden * (1.0 - sigmoid_value))

def reference(user_rows, projection, item_table, positive, negatives):
    score_scale = 4.0 / math.sqrt(D)
    per_group = user_rows.shape[0] // N_GRP
    item_grad = jnp.zeros(item_table.shape, jnp.float32)
    user_parts = []
    for group_index in range(N_GRP):
        user_block = user_rows[group_index * per_group:(group_index + 1) * per_group]
        pos_ids = positive[group_index * per_group:(group_index + 1) * per_group]
        neg_ids = negatives[group_index]
        hidden = jnp.dot(user_block, projection, preferred_element_type=jnp.float32)
        hidden_z = jax.nn.silu(hidden).astype(jnp.bfloat16)
        neg_table = item_table[neg_ids]
        pos_rows = item_table[pos_ids]
        neg_logits = score_scale * jnp.dot(hidden_z, neg_table.T, preferred_element_type=jnp.float32)
        pos_logit = score_scale * lax.optimization_barrier(jnp.sum(hidden_z.astype(jnp.float32) * pos_rows.astype(jnp.float32), axis=1))
        row_max = jnp.maximum(pos_logit, lax.optimization_barrier(jnp.max(neg_logits, axis=1)))
        exp_total = jnp.exp(pos_logit - row_max) + lax.optimization_barrier(jnp.sum(jnp.exp(neg_logits - row_max[:, None]), axis=1))
        log_total = row_max + jnp.log(exp_total)
        neg_prob = jnp.exp(neg_logits - log_total[:, None]).astype(jnp.bfloat16)
        pos_weight = jnp.exp(pos_logit - log_total) - 1.0
        grad_z = score_scale * (jnp.dot(neg_prob, neg_table, preferred_element_type=jnp.float32) + pos_weight[:, None] * pos_rows.astype(jnp.float32))
        grad_hidden = (grad_z * silu_slope(hidden)).astype(jnp.bfloat16)
        user_parts.append(jnp.dot(grad_hidden, projection.T, preferred_element_type=jnp.float32).astype(jnp.bfloat16))
        neg_term = score_scale * jnp.dot(neg_prob.T, hidden_z, preferred_element_type=jnp.float32)
        pos_term = (score_scale * pos_weight)[:, None] * hidden_z.astype(jnp.float32)
        item_grad = item_grad.at[neg_ids].add(neg_term).at[pos_ids].add(pos_term)
    return (jnp.concatenate(user_parts, axis=0), item_grad)
```

```python
import functools
import math

import jax
import jax.numpy as jnp
from jax import lax
from jax.experimental import pallas as pl
from jax.experimental.pallas import tpu as pltpu
from jax.sharding import PartitionSpec as P

MESH = pl.DeviceIdType.MESH
BF, F32, I32 = jnp.bfloat16, jnp.float32, jnp.int32
W = 2048
HALF = W // 2
CH = 512
NC = W // CH
ROWS = 64
USERS = 128
SLOTS = 16
RING = (0, 1, -1, 2)
PLACE = {0: 0, 1: 1, -1: 2, 2: 3}
FULL, LEFT, RIGHT = pl.ds(0, W), pl.ds(0, HALF), pl.ds(HALF, HALF)


def fold(v):
    return {-3: 1, -2: 2, 3: -1}.get(v, v)


def dot(a, b, ca=1, cb=0):
    return lax.dot_general(a, b, (((ca,), (cb,)), ((), ())), preferred_element_type=F32)


def kernel(
    user_hbm, proj_hbm, tab, pos_lane, pos_col, neg_col, neg_lane, ug_ref, ig_ref,
    users, proj, hidden, z_ref, gh, probs, logits, pos_rows,
    shards, table, ids, pick_ref, slot_of, slot_to, send_slots, recv_slots, send_grads, recv_grads,
    back, back_in, xs, xr, part, sib_in, r_left, r_right, r_a, r_b,
    load_sem, ids_sem, shard_sem, slot_sem, grad_sem, back_sem, x_sem,
    ag_send, ag_recv, sib_send, sib_recv, rs_send, rs_recv,
):
    scale = 4.0 / math.sqrt(W)
    g, m = lax.axis_index("grp"), lax.axis_index("mem")
    c, y, zz = lax.rem(m, 2), lax.rem(m // 2, 4), m // 8
    me = (g * 4 + zz) * 2 + c

    def dev(gx, dz, dy, cc):
        return (gx, (lax.rem(zz + dz + 4, 4) * 4 + lax.rem(y + dy + 4, 4)) * 2 + cc)

    def mate(i):
        u = lax.rem(me + i, 32)
        return u, (u // 8, (lax.rem(u // 2, 4) * 4 + y) * 2 + lax.rem(u, 2))

    def xpeer(i):
        gx = lax.rem(g + i, 4)
        return gx, (gx, m)

    sib = dev(g, 0, 0, 1 - c)
    late = []

    def remote(src, dst, s_sem, r_sem, to):
        cp = pltpu.make_async_remote_copy(
            src_ref=src, dst_ref=dst, send_sem=s_sem, recv_sem=r_sem, device_id=to, device_id_type=MESH
        )
        cp.start()
        return cp

    def arrive(ref, sem):
        pltpu.make_async_copy(ref, ref, sem).wait()

    barrier = pltpu.get_barrier_semaphore()

    def greet(i, carry):
        pl.semaphore_signal(barrier, inc=1, device_id=mate(i)[1], device_id_type=MESH)
        return carry

    lax.fori_loop(1, 32, greet, 0)
    for dy in (1, 2, 3):
        pl.semaphore_signal(barrier, inc=1, device_id=dev(g, 0, dy, c), device_id_type=MESH)

    loads = [pltpu.make_async_copy(user_hbm, users, load_sem.at[0])]
    for t in range(NC):
        cols = pl.ds(t * CH, CH)
        loads.append(pltpu.make_async_copy(proj_hbm.at[:, cols], proj.at[:, cols], load_sem.at[1 + t]))
    for cp in loads:
        cp.start()

    pick = (neg_col[...] == lax.broadcasted_iota(I32, (32, ROWS), 1)).astype(BF)
    picked = dot(pick, tab[...])
    for gi in range(4):
        rows8 = picked[8 * gi:8 * gi + 8, :]
        xs[gi] = jnp.concatenate([rows8[:, :HALF], rows8[:, HALF:]], axis=0).astype(BF)
    my_shard = pl.ds(pl.multiple_of(y * ROWS, ROWS), ROWS)
    shards[my_shard, :] = tab[...]
    ids[me] = pos_lane[...]
    pl.semaphore_wait(barrier, 34)

    for i in (1, 2, 3):
        gx, to = xpeer(i)
        late.append(remote(xs.at[gx], xr.at[g], x_sem.at[0], x_sem.at[1], to))
    xr[g] = xs[g]

    def send_ids(i, carry):
        remote(pos_lane, ids.at[me], ids_sem.at[0], ids_sem.at[1], mate(i)[1])
        return carry

    lax.fori_loop(1, 32, send_ids, 0)
    for t in range(NC):
        for dy in (1, 3, 2):
            cols = pl.ds(t * CH, CH)
            remote(tab.at[:, cols], shards.at[my_shard, cols], shard_sem.at[0, t], shard_sem.at[1, t], dev(g, 0, dy, c))

    def block(cc, dz, dy):
        at = ((cc * 4 + lax.rem(zz + dz + 4, 4)) * 4 + lax.rem(y + dy + 4, 4)) * 32
        return pl.ds(pl.multiple_of(at, 32), 32)

    def sem_at(f, s, p):
        return (PLACE[f] * 4 + PLACE[s]) * 2 + p

    count = [0]

    def push(f, s, cols, along_z, sgn, p):
        nf, ns = (fold(f - sgn), s) if along_z else (f, fold(s - sgn))
        ref = table.at[block(c, f, s), cols]
        to = dev(g, sgn, 0, c) if along_z else dev(g, 0, sgn, c)
        late.append(remote(ref, ref, ag_send.at[count[0]], ag_recv.at[sem_at(nf, ns, p)], to))
        count[0] += 1

    across = []

    def over(f, s, cols, p):
        ref = table.at[block(c, f, s), cols]
        k = sem_at(f, s, p)
        late.append(remote(ref, ref, sib_send.at[k], sib_recv.at[k], sib))
        across.append((f, s, cols, p))

    def here(f, s, cols, p):
        arrive(table.at[block(c, f, s), cols], ag_recv.at[sem_at(f, s, p)])

    def second(f, cols, p):
        push(f, 0, cols, False, 1, p)
        push(f, 0, cols, False, -1, p)
        over(f, 0, cols, p)

    def relay(f, parts):
        for cols, p in parts:
            for s in (-1, 1):
                here(f, s, cols, p)
                over(f, s, cols, p)
        push(f, -1, LEFT, False, 1, 0)
        push(f, 1, RIGHT, False, -1, 1)

    arrive(xr.at[pl.ds(0, 3)], x_sem.at[1])
    lines = []
    for gi in range(4):
        v = xr[gi].astype(F32)
        lines.append(jnp.concatenate([v[:8], v[8:]], axis=1))
    table[block(c, 0, 0), :] = jnp.concatenate(lines, axis=0).astype(BF)
    push(0, 0, FULL, True, 1, 0)
    push(0, 0, FULL, True, -1, 0)
    second(0, FULL, 0)

    lane = lax.broadcasted_iota(I32, (USERS, USERS), 1)
    sub = lax.broadcasted_iota(I32, (USERS, USERS), 0)
    own_c, own_l = pos_col[...] >> 6, pos_lane[...] >> 6
    same = own_c == own_l
    rank_c = jnp.sum((same & (lane < sub)).astype(F32), axis=1, keepdims=True).astype(I32)
    rank_l = jnp.sum((same & (sub < lane)).astype(F32), axis=0, keepdims=True).astype(I32)

    def slot(o, rank):
        relay_of = ((o >> 5) * 4 + ((o >> 3) & 3)) * 2 + (o & 1)
        return relay_of * SLOTS + ((o >> 1) & 3) * 4 + rank

    slot_of[...] = (slot(own_c, rank_c) == lax.broadcasted_iota(I32, (USERS, 512), 1)).astype(BF)
    slot_to[...] = (slot(own_l, rank_l) == lax.broadcasted_iota(I32, (512, USERS), 0)).astype(BF)

    arrive(ids.at[pl.ds(0, 31)], ids_sem.at[1])
    wide = jnp.broadcast_to(ids[...], (32, SLOTS, USERS)).reshape(512, USERS)
    s_iota = lax.broadcasted_iota(I32, (512, USERS), 0) & (SLOTS - 1)
    owner_q = g * 32 + (zz * 4 + (s_iota >> 2)) * 2 + c
    hit = (wide >> 6) == owner_q
    before = dot(hit.astype(BF), (sub < lane).astype(BF))
    take = hit & (before == (s_iota & 3).astype(F32))
    found = jnp.sum(jnp.where(take, (wide & 63) + 1, 0).astype(F32), axis=1, keepdims=True).astype(I32)
    q_col = (lax.broadcasted_iota(I32, (512, 1), 0) & (SLOTS - 1)) >> 2
    target = jnp.where(found > 0, q_col * ROWS + found - 1, -1)
    pick_ref[...] = (target == lax.broadcasted_iota(I32, (512, 256), 1)).astype(BF)

    def my_slots(u):
        return pl.ds(pl.multiple_of(u * SLOTS, SLOTS), SLOTS)

    def gather(t):
        cols = pl.ds(t * CH, CH)
        arrive(shards.at[pl.ds(0, 192), cols], shard_sem.at[1, t])
        send_slots[:, cols] = dot(pick_ref[...], shards[:, cols]).astype(BF)

        def out(i, carry):
            u, to = mate(i)
            remote(send_slots.at[my_slots(u), cols], recv_slots.at[my_slots(me), cols], slot_sem.at[0, t], slot_sem.at[1, t], to)
            return carry

        lax.fori_loop(1, 32, out, 0)
        recv_slots[my_slots(me), cols] = send_slots[my_slots(me), cols]

    def project(t):
        cols = pl.ds(t * CH, CH)
        loads[1 + t].wait()
        h = dot(users[...], proj[:, cols])
        hidden[:, cols] = h
        z_ref[:, cols] = (h * jax.nn.sigmoid(h)).astype(BF)

    here(-1, 0, FULL, 0)
    push(-1, 0, LEFT, True, 1, 0)
    here(1, 0, FULL, 0)
    push(1, 0, RIGHT, True, -1, 1)
    second(-1, FULL, 0)
    second(1, FULL, 0)
    gather(0)
    relay(0, [(FULL, 0)])
    gather(1)
    here(2, 0, LEFT, 0)
    second(2, LEFT, 0)
    here(2, 0, RIGHT, 1)
    second(2, RIGHT, 1)
    loads[0].wait()
    project(0)
    gather(2)
    relay(-1, [(FULL, 0)])
    project(1)
    relay(1, [(FULL, 0)])
    gather(3)
    project(2)
    relay(2, [(LEFT, 0), (RIGHT, 1)])
    project(3)
    for f in RING:
        here(f, 2, LEFT, 0)
        over(f, 2, LEFT, 0)
        here(f, 2, RIGHT, 1)
        over(f, 2, RIGHT, 1)

    def log_rows(cc):
        for t in range(2):
            rows = pl.ds(pl.multiple_of(cc * 512 + t * 256, 256), 256)
            logits[:, rows] = scale * dot(z_ref[...], table[rows, :], 1, 1)

    log_rows(c)
    for f, s, cols, p in across:
        arrive(table.at[block(1 - c, f, s), cols], sib_recv.at[sem_at(f, s, p)])
    log_rows(1 - c)
    pos_logit = jnp.zeros((USERS, 1), F32)
    for t in range(NC):
        cols = pl.ds(t * CH, CH)
        arrive(recv_slots.at[pl.ds(0, 31 * SLOTS), cols], slot_sem.at[1, t])
        pr = dot(slot_of[...], recv_slots[:, cols])
        pos_rows[:, cols] = pr
        pos_logit = pos_logit + jnp.sum(z_ref[:, cols].astype(F32) * pr, axis=1, keepdims=True)
    pos_logit = scale * pos_logit
    lg = logits[...]
    top = jnp.maximum(pos_logit, jnp.max(lg, axis=1, keepdims=True))
    total = jnp.exp(pos_logit - top) + jnp.sum(jnp.exp(lg - top), axis=1, keepdims=True)
    log_total = top + jnp.log(total)
    probs[...] = jnp.exp(lg - log_total).astype(BF)
    pos_weight = jnp.exp(pos_logit - log_total) - 1.0

    for t in range(NC):
        cols = pl.ds(t * CH, CH)
        term = ((scale * pos_weight) * z_ref[:, cols].astype(F32)).astype(BF)
        send_grads[:, cols] = dot(slot_to[...], term).astype(BF)

        def out(i, carry, cols=cols, t=t):
            u, to = mate(i)
            remote(send_grads.at[my_slots(u), cols], recv_grads.at[my_slots(me), cols], grad_sem.at[0, t], grad_sem.at[1, t], to)
            return carry

        lax.fori_loop(1, 32, out, 0)
        recv_grads[my_slots(me), cols] = send_grads[my_slots(me), cols]

    def line(cc, dz):
        return pl.ds(pl.multiple_of((cc * 4 + lax.rem(zz + dz + 4, 4)) * 128, 128), 128)

    ORDER = (2, 1, -1, 0)
    for i, dz in enumerate(ORDER):
        for cc in (1 - c, c):
            rows = line(cc, dz)
            pt = probs[:, rows]
            for t in range(NC):
                cols = pl.ds(t * CH, CH)
                part[rows, cols] = (scale * dot(pt, z_ref[:, cols], 0, 0)).astype(BF)
        late.append(remote(part.at[line(1 - c, dz)], sib_in.at[i], rs_send.at[i], rs_recv.at[i], sib))

    rs_count = [4]

    def push_sum(src, dst, k, to):
        late.append(remote(src, dst, rs_send.at[rs_count[0]], rs_recv.at[k], to))
        rs_count[0] += 1

    def ring(i, rows, to):
        def first():
            push_sum(part.at[rows(2), LEFT], r_left.at[i], 4 + 4 * i, to(-1))
            push_sum(part.at[rows(2), RIGHT], r_right.at[i], 5 + 4 * i, to(1))

        def middle():
            arrive(r_left.at[i], rs_recv.at[4 + 4 * i])
            r = rows(-1)
            part[r, LEFT] = (part[r, LEFT].astype(F32) + r_left[i].astype(F32)).astype(BF)
            push_sum(part.at[r], r_a.at[i], 6 + 4 * i, to(-1))
            arrive(r_right.at[i], rs_recv.at[5 + 4 * i])
            r = rows(1)
            part[r, RIGHT] = (part[r, RIGHT].astype(F32) + r_right[i].astype(F32)).astype(BF)
            push_sum(part.at[r], r_b.at[i], 7 + 4 * i, to(1))

        def last():
            arrive(r_a.at[i], rs_recv.at[6 + 4 * i])
            arrive(r_b.at[i], rs_recv.at[7 + 4 * i])
            r = rows(0)
            return part[r, :].astype(F32) + r_a[i].astype(F32) + r_b[i].astype(F32)

        return first, middle, last

    rings = []
    for i, dz in enumerate(ORDER):
        arrive(sib_in.at[i], rs_recv.at[i])
        rows = line(c, dz)
        part[rows, :] = (part[rows, :].astype(F32) + sib_in[i].astype(F32)).astype(BF)
        rings.append(ring(i, lambda d, dz=dz: block(c, dz, d), lambda s: dev(g, 0, s, c)))
        rings[i][0]()

    def slope(t):
        cols = pl.ds(t * CH, CH)
        h = hidden[:, cols]
        sg = jax.nn.sigmoid(h)
        gz = scale * (dot(probs[...], table[:, cols]) + pos_weight * pos_rows[:, cols])
        gh[:, cols] = (gz * (sg * (1.0 + h * (1.0 - sg)))).astype(BF)

    def user(t):
        rows = pl.ds(t * CH, CH)
        ug_ref[:, rows] = dot(gh[...], proj[rows, :], 1, 1).astype(BF)

    def gather_back(t):
        cols = pl.ds(t * CH, CH)
        arrive(recv_grads.at[pl.ds(0, 31 * SLOTS), cols], grad_sem.at[1, t])
        back[:, cols] = dot(pick_ref[...], recv_grads[:, cols], 0, 0).astype(BF)
        for dy in (1, 3, 2):
            src = pl.ds(pl.multiple_of(lax.rem(y + dy, 4) * ROWS, ROWS), ROWS)
            remote(back.at[src, cols], back_in.at[my_shard, cols], back_sem.at[0, t], back_sem.at[1, t], dev(g, 0, dy, c))
        back_in[my_shard, cols] = back[my_shard, cols]

    slope(0)
    rings[0][1]()
    slope(1)
    rings[1][1]()
    slope(2)
    rings[2][1]()
    slope(3)
    rings[3][1]()
    gather_back(0)
    lineup = ring(4, lambda d: block(c, d, 0), lambda s: dev(g, s, 0, c))

    def settle(i):
        part[block(c, ORDER[i], 0), :] = rings[i][2]().astype(BF)

    settle(0)
    lineup[0]()
    user(0)
    settle(1)
    settle(2)
    gather_back(1)
    lineup[1]()
    user(1)
    gather_back(2)
    mine = rings[3][2]()
    part[block(c, 0, 0), :] = mine.astype(BF)
    share = lineup[2]()
    for gi in range(4):
        rows8 = share[8 * gi:8 * gi + 8, :]
        xs[4 + gi] = jnp.concatenate([rows8[:, :HALF], rows8[:, HALF:]], axis=0).astype(BF)
    for i in (1, 2, 3):
        gx, to = xpeer(i)
        late.append(remote(xs.at[4 + gx], xr.at[4 + g], x_sem.at[2], x_sem.at[3], to))
    xr[4 + g] = xs[4 + g]
    gather_back(3)
    user(2)
    user(3)
    arrive(xr.at[pl.ds(4, 3)], x_sem.at[3])
    lines = []
    for gi in range(4):
        v = xr[4 + gi].astype(F32)
        lines.append(jnp.concatenate([v[:8], v[8:]], axis=1))
    returned = jnp.concatenate(lines, axis=0).astype(BF)
    place = (neg_lane[...] == lax.broadcasted_iota(I32, (ROWS, 32), 0)).astype(BF)
    for t in range(NC):
        cols = pl.ds(t * CH, CH)
        arrive(back_in.at[pl.ds(0, 192), cols], back_sem.at[1, t])
        acc = dot(place, returned[:, t * CH:(t + 1) * CH])
        for q in range(4):
            acc = acc + back_in[pl.ds(q * ROWS, ROWS), cols].astype(F32)
        ig_ref[:, cols] = acc

    for cp in late[:3]:
        pass
    arrive(xs.at[pl.ds(0, 3)], x_sem.at[0])
    arrive(xs.at[pl.ds(4, 3)], x_sem.at[2])
    arrive(ids.at[pl.ds(0, 31)], ids_sem.at[0])
    for t in range(NC):
        cols = pl.ds(t * CH, CH)
        arrive(shards.at[pl.ds(0, 192), cols], shard_sem.at[0, t])
        arrive(send_slots.at[pl.ds(0, 31 * SLOTS), cols], slot_sem.at[0, t])
        arrive(send_grads.at[pl.ds(0, 31 * SLOTS), cols], grad_sem.at[0, t])
        arrive(back.at[pl.ds(0, 192), cols], back_sem.at[0, t])
    for cp in late[3:-3]:
        cp.wait_send()


def on_device(user_rows, projection, item_table, positive, negatives):
    first_row = lax.axis_index(("grp", "mem")) * ROWS
    local = negatives - first_row
    vm = pl.BlockSpec(memory_space=pltpu.VMEM)
    hbm = pl.BlockSpec(memory_space=pl.ANY)
    dma = pltpu.SemaphoreType.DMA
    v = pltpu.VMEM
    return pl.pallas_call(
        kernel,
        out_shape=(jax.ShapeDtypeStruct((USERS, W), BF), jax.ShapeDtypeStruct((ROWS, W), F32)),
        in_specs=[hbm, hbm, vm, vm, vm, vm, vm],
        out_specs=(vm, vm),
        scratch_shapes=[
            v((USERS, W), BF), v((W, W), BF), v((USERS, W), F32), v((USERS, W), BF), v((USERS, W), BF),
            v((USERS, 1024), BF), v((USERS, 1024), F32), v((USERS, W), F32),
            v((256, W), BF), v((1024, W), BF), v((32, 1, USERS), I32), v((512, 256), BF),
            v((USERS, 512), BF), v((512, USERS), BF),
            v((512, W), BF), v((512, W), BF), v((512, W), BF), v((512, W), BF),
            v((256, W), BF), v((256, W), BF), v((8, 16, HALF), BF), v((8, 16, HALF), BF),
            v((1024, W), BF), v((4, 128, W), BF),
            v((5, 32, HALF), BF), v((5, 32, HALF), BF), v((5, 32, W), BF), v((5, 32, W), BF),
            dma((5,)), dma((2,)), dma((2, NC)), dma((2, NC)), dma((2, NC)), dma((2, NC)), dma((4,)),
            dma((40,)), dma((32,)), dma((32,)), dma((32,)), dma((24,)), dma((24,)),
        ],
        compiler_params=pltpu.CompilerParams(collective_id=0, has_side_effects=True, vmem_limit_bytes=58 << 20),
        cost_estimate=pl.CostEstimate(flops=5 * 10**9, bytes_accessed=12 * 2**20, transcendentals=10**6),
    )(
        user_rows,
        projection,
        item_table,
        positive.reshape(1, USERS),
        positive.reshape(USERS, 1),
        local.reshape(32, 1),
        local.reshape(1, 32),
    )


def solution(mesh):
    placed = (
        P(("grp", "mem"), None),
        P(),
        P(("grp", "mem"), None),
        P(("grp", "mem")),
        P(None, ("grp", "mem")),
    )
    return jax.shard_map(
        on_device,
        mesh=mesh,
        in_specs=placed,
        out_specs=(P(("grp", "mem"), None), P(("grp", "mem"), None)),
        check_vma=False,
    )
```

```python
import functools
import math

import jax
import jax.numpy as jnp
from jax import lax
from jax.experimental import pallas as pl
from jax.experimental.pallas import tpu as pltpu
from jax.sharding import PartitionSpec as P

MESH = pl.DeviceIdType.MESH
BF, F32, I32 = jnp.bfloat16, jnp.float32, jnp.int32
W = 2048
HALF = W // 2
CH = 512
NC = W // CH
EARLY = 4
ROWS = 64
USERS = 128
SLOTS = 16
RING = (0, 1, -1, 2)
PLACE = {0: 0, 1: 1, -1: 2, 2: 3}
FULL, LEFT, RIGHT = pl.ds(0, W), pl.ds(0, HALF), pl.ds(HALF, HALF)


def fold(v):
    return {-3: 1, -2: 2, 3: -1}.get(v, v)


def dot(a, b, ca=1, cb=0):
    return lax.dot_general(a, b, (((ca,), (cb,)), ((), ())), preferred_element_type=F32)


def kernel(
    user_hbm, proj_hbm, tab_hbm, pos_hbm, neg_hbm, ug_ref, ig_ref,
    tab, neg_ids, users, proj, hidden, z_ref, gh, probs, logits, pos_rows,
    shards, table, ids, pick_ref, slot_of, slot_to, send_slots, recv_slots, send_grads, recv_grads,
    take_ref, weight_out, weights, back, back_in, xs, xr, part, sib_in, r_left, r_right, r_a, r_b,
    load_sem, ids_sem, weight_sem, shard_sem, slot_sem, grad_sem, back_sem, x_sem,
    ag_send, ag_recv, sib_send, sib_recv, rs_send, rs_recv,
):
    scale = 4.0 / math.sqrt(W)
    g, m = lax.axis_index("grp"), lax.axis_index("mem")
    c, y, zz = lax.rem(m, 2), lax.rem(m // 2, 4), m // 8
    me = (g * 4 + zz) * 2 + c

    def dev(gx, dz, dy, cc):
        return (gx, (lax.rem(zz + dz + 4, 4) * 4 + lax.rem(y + dy + 4, 4)) * 2 + cc)

    def mate(i):
        p = i // 2
        ux, uz, uc = lax.rem(g + p // 4 + p, 4), lax.rem(zz + p, 4), lax.rem(c + i, 2)
        return (ux * 4 + uz) * 2 + uc, (ux, (uz * 4 + y) * 2 + uc)

    def xpeer(i):
        gx = lax.rem(g + i, 4)
        return gx, (gx, m)

    sib = dev(g, 0, 0, 1 - c)
    late = []

    def remote(src, dst, s_sem, r_sem, to):
        cp = pltpu.make_async_remote_copy(
            src_ref=src, dst_ref=dst, send_sem=s_sem, recv_sem=r_sem, device_id=to, device_id_type=MESH
        )
        cp.start()
        return cp

    def arrive(ref, sem):
        pltpu.make_async_copy(ref, ref, sem).wait()

    barrier = pltpu.get_barrier_semaphore()

    def greet(i, carry):
        pl.semaphore_signal(barrier, inc=1, device_id=mate(i)[1], device_id_type=MESH)
        return carry

    lax.fori_loop(1, 32, greet, 0)
    for dy in (1, 2, 3):
        pl.semaphore_signal(barrier, inc=1, device_id=dev(g, 0, dy, c), device_id_type=MESH)

    first_loads = [
        pltpu.make_async_copy(tab_hbm, tab, load_sem.at[5]),
        pltpu.make_async_copy(neg_hbm, neg_ids, load_sem.at[6]),
        pltpu.make_async_copy(pos_hbm, ids.at[me], load_sem.at[7]),
    ]
    for cp in first_loads:
        cp.start()
    loads = [pltpu.make_async_copy(user_hbm, users, load_sem.at[0])]
    for t in range(NC):
        cols = pl.ds(t * CH, CH)
        loads.append(pltpu.make_async_copy(proj_hbm.at[:, cols], proj.at[:, cols], load_sem.at[1 + t]))
    for cp in loads:
        cp.start()

    for cp in first_loads:
        cp.wait()
    pos_lane = ids.at[me]

    diagonal = lax.broadcasted_iota(I32, (8, 8), 0) == lax.broadcasted_iota(I32, (8, 8), 1)
    columns = []
    for gi in range(4):
        wide_ids = jnp.broadcast_to(neg_ids[gi:gi + 1, :], (8, 8)).astype(F32)
        columns.append(jnp.sum(jnp.where(diagonal, wide_ids, 0.0), axis=1, keepdims=True))
    neg_col = jnp.concatenate(columns, axis=0).astype(I32) - (g * 32 + m) * ROWS
    pick = (neg_col == lax.broadcasted_iota(I32, (32, ROWS), 1)).astype(BF)
    picked = dot(pick, tab[...])
    for gi in range(4):
        rows8 = picked[8 * gi:8 * gi + 8, :]
        xs[gi] = jnp.concatenate([rows8[:, :HALF], rows8[:, HALF:]], axis=0).astype(BF)
    my_shard = pl.ds(pl.multiple_of(y * ROWS, ROWS), ROWS)
    shards[my_shard, :] = tab[...]
    pl.semaphore_wait(barrier, 34)

    for i in (1, 2, 3):
        gx, to = xpeer(i)
        late.append(remote(xs.at[gx], xr.at[g], x_sem.at[0], x_sem.at[1], to))
    xr[g] = xs[g]

    def send_ids(i, carry):
        remote(pos_lane, ids.at[me], ids_sem.at[0], ids_sem.at[1], mate(i)[1])
        return carry

    lax.fori_loop(1, 32, send_ids, 0)
    for t in range(NC):
        for dy in (1, 3, 2):
            cols = pl.ds(t * CH, CH)
            remote(tab.at[:, cols], shards.at[my_shard, cols], shard_sem.at[0, t], shard_sem.at[1, t], dev(g, 0, dy, c))

    def block(cc, dz, dy):
        at = ((cc * 4 + lax.rem(zz + dz + 4, 4)) * 4 + lax.rem(y + dy + 4, 4)) * 32
        return pl.ds(pl.multiple_of(at, 32), 32)

    def sem_at(f, s, p):
        return (PLACE[f] * 4 + PLACE[s]) * 2 + p

    count = [0]

    def push(f, s, cols, along_z, sgn, p):
        nf, ns = (fold(f - sgn), s) if along_z else (f, fold(s - sgn))
        ref = table.at[block(c, f, s), cols]
        to = dev(g, sgn, 0, c) if along_z else dev(g, 0, sgn, c)
        late.append(remote(ref, ref, ag_send.at[count[0]], ag_recv.at[sem_at(nf, ns, p)], to))
        count[0] += 1

    across = []

    def over(f, s, cols, p):
        ref = table.at[block(c, f, s), cols]
        k = sem_at(f, s, p)
        late.append(remote(ref, ref, sib_send.at[k], sib_recv.at[k], sib))
        across.append((f, s, cols, p))

    def here(f, s, cols, p):
        arrive(table.at[block(c, f, s), cols], ag_recv.at[sem_at(f, s, p)])

    def second(f, cols, p):
        push(f, 0, cols, False, 1, p)
        push(f, 0, cols, False, -1, p)
        over(f, 0, cols, p)

    def relay(f, parts):
        for cols, p in parts:
            for s in (-1, 1):
                here(f, s, cols, p)
                over(f, s, cols, p)
        push(f, -1, LEFT, False, 1, 0)
        push(f, 1, RIGHT, False, -1, 1)

    arrive(xr.at[pl.ds(0, 3)], x_sem.at[1])
    lines = []
    for gi in range(4):
        v = xr[gi].astype(F32)
        lines.append(jnp.concatenate([v[:8], v[8:]], axis=1))
    table[block(c, 0, 0), :] = jnp.concatenate(lines, axis=0).astype(BF)
    push(0, 0, FULL, True, 1, 0)
    push(0, 0, FULL, True, -1, 0)
    second(0, FULL, 0)

    lane = lax.broadcasted_iota(I32, (USERS, USERS), 1)
    sub = lax.broadcasted_iota(I32, (USERS, USERS), 0)
    own_l = pos_lane[...] >> 6
    own_c = jnp.sum(jnp.where(lane == sub, own_l.astype(F32), 0.0), axis=1, keepdims=True).astype(I32)
    same = own_c == own_l
    rank_c = jnp.sum((same & (lane < sub)).astype(F32), axis=1, keepdims=True).astype(I32)
    rank_l = jnp.sum((same & (sub < lane)).astype(F32), axis=0, keepdims=True).astype(I32)

    def slot(o, rank):
        relay_of = ((o >> 5) * 4 + ((o >> 3) & 3)) * 2 + (o & 1)
        return relay_of * SLOTS + ((o >> 1) & 3) * 4 + rank

    slot_of[...] = (slot(own_c, rank_c) == lax.broadcasted_iota(I32, (USERS, 512), 1)).astype(BF)
    slot_to[...] = (slot(own_l, rank_l) == lax.broadcasted_iota(I32, (512, USERS), 0)).astype(BF)

    arrive(ids.at[pl.ds(0, 31)], ids_sem.at[1])
    wide = jnp.broadcast_to(ids[...], (32, SLOTS, USERS)).reshape(512, USERS)
    s_iota = lax.broadcasted_iota(I32, (512, USERS), 0) & (SLOTS - 1)
    owner_q = g * 32 + (zz * 4 + (s_iota >> 2)) * 2 + c
    hit = (wide >> 6) == owner_q
    before = dot(hit.astype(BF), (sub < lane).astype(BF))
    take = hit & (before == (s_iota & 3).astype(F32))
    take_ref[...] = take.astype(F32)
    found = jnp.sum(jnp.where(take, (wide & 63) + 1, 0).astype(F32), axis=1, keepdims=True).astype(I32)
    q_col = (lax.broadcasted_iota(I32, (512, 1), 0) & (SLOTS - 1)) >> 2
    target = jnp.where(found > 0, q_col * ROWS + found - 1, -1)
    pick_ref[...] = (target == lax.broadcasted_iota(I32, (512, 256), 1)).astype(BF)

    def my_slots(u):
        return pl.ds(pl.multiple_of(u * SLOTS, SLOTS), SLOTS)

    def gather(t):
        cols = pl.ds(t * CH, CH)
        arrive(shards.at[pl.ds(0, 192), cols], shard_sem.at[1, t])
        send_slots[:, cols] = dot(pick_ref[...], shards[:, cols]).astype(BF)

        def out(i, carry):
            u, to = mate(i)
            remote(send_slots.at[my_slots(u), cols], recv_slots.at[my_slots(me), cols], slot_sem.at[0, t], slot_sem.at[1, t], to)
            return carry

        lax.fori_loop(1, 32, out, 0)
        recv_slots[my_slots(me), cols] = send_slots[my_slots(me), cols]

    def project(t):
        cols = pl.ds(t * CH, CH)
        loads[1 + t].wait()
        h = dot(users[...], proj[:, cols])
        hidden[:, cols] = h
        z_ref[:, cols] = (h * jax.nn.sigmoid(h)).astype(BF)

    def send_z(t):
        cols = pl.ds(t * CH, CH)
        send_grads[:, cols] = dot(slot_to[...], z_ref[:, cols]).astype(BF)

        def out(i, carry):
            u, to = mate(i)
            remote(send_grads.at[my_slots(u), cols], recv_grads.at[my_slots(me), cols], grad_sem.at[0, t], grad_sem.at[1, t], to)
            return carry

        lax.fori_loop(1, 32, out, 0)
        recv_grads[my_slots(me), cols] = send_grads[my_slots(me), cols]

    loads[0].wait()
    for t in range(NC):
        project(t)
    here(-1, 0, FULL, 0)
    push(-1, 0, LEFT, True, 1, 0)
    here(1, 0, FULL, 0)
    push(1, 0, RIGHT, True, -1, 1)
    second(-1, FULL, 0)
    second(1, FULL, 0)
    gather(0)
    relay(0, [(FULL, 0)])
    gather(1)
    here(2, 0, LEFT, 0)
    second(2, LEFT, 0)
    here(2, 0, RIGHT, 1)
    second(2, RIGHT, 1)
    gather(2)
    relay(-1, [(FULL, 0)])
    gather(3)
    relay(1, [(FULL, 0)])
    relay(2, [(LEFT, 0), (RIGHT, 1)])
    for t in range(EARLY):
        send_z(t)
    for f in RING:
        here(f, 2, LEFT, 0)
        over(f, 2, LEFT, 0)
        here(f, 2, RIGHT, 1)
        over(f, 2, RIGHT, 1)

    def log_rows(cc):
        for t in range(2):
            rows = pl.ds(pl.multiple_of(cc * 512 + t * 256, 256), 256)
            logits[:, rows] = scale * dot(z_ref[...], table[rows, :], 1, 1)

    log_rows(c)
    for f, s, cols, p in across:
        arrive(table.at[block(1 - c, f, s), cols], sib_recv.at[sem_at(f, s, p)])
    log_rows(1 - c)
    pos_logit = jnp.zeros((USERS, 1), F32)
    for t in range(NC):
        cols = pl.ds(t * CH, CH)
        arrive(recv_slots.at[pl.ds(0, 31 * SLOTS), cols], slot_sem.at[1, t])
        pr = dot(slot_of[...], recv_slots[:, cols])
        pos_rows[:, cols] = pr
        pos_logit = pos_logit + jnp.sum(z_ref[:, cols].astype(F32) * pr, axis=1, keepdims=True)
    pos_logit = scale * pos_logit
    lg = logits[...]
    top = jnp.maximum(pos_logit, jnp.max(lg, axis=1, keepdims=True))
    total = jnp.exp(pos_logit - top) + jnp.sum(jnp.exp(lg - top), axis=1, keepdims=True)
    log_total = top + jnp.log(total)
    probs[...] = jnp.exp(lg - log_total).astype(BF)
    pos_weight = jnp.exp(pos_logit - log_total) - 1.0

    weight_out[...] = jnp.sum(jnp.where(lane == sub, pos_weight, 0.0), axis=0, keepdims=True)
    weights[me] = weight_out[...]

    def send_weights(i, carry):
        remote(weight_out, weights.at[me], weight_sem.at[0], weight_sem.at[1], mate(i)[1])
        return carry

    lax.fori_loop(1, 32, send_weights, 0)
    for t in range(EARLY, NC):
        send_z(t)

    def line(cc, dz):
        return pl.ds(pl.multiple_of((cc * 4 + lax.rem(zz + dz + 4, 4)) * 128, 128), 128)

    ORDER = (2, 1, -1, 0)
    for i, dz in enumerate(ORDER):
        for cc in (1 - c, c):
            rows = line(cc, dz)
            pt = probs[:, rows]
            for t in range(NC):
                cols = pl.ds(t * CH, CH)
                part[rows, cols] = (scale * dot(pt, z_ref[:, cols], 0, 0)).astype(BF)
        late.append(remote(part.at[line(1 - c, dz)], sib_in.at[i], rs_send.at[i], rs_recv.at[i], sib))

    rs_count = [4]

    def push_sum(src, dst, k, to):
        late.append(remote(src, dst, rs_send.at[rs_count[0]], rs_recv.at[k], to))
        rs_count[0] += 1

    def ring(i, rows, to):
        def first():
            push_sum(part.at[rows(2), LEFT], r_left.at[i], 4 + 4 * i, to(-1))
            push_sum(part.at[rows(2), RIGHT], r_right.at[i], 5 + 4 * i, to(1))

        def middle():
            arrive(r_left.at[i], rs_recv.at[4 + 4 * i])
            r = rows(-1)
            part[r, LEFT] = (part[r, LEFT].astype(F32) + r_left[i].astype(F32)).astype(BF)
            push_sum(part.at[r], r_a.at[i], 6 + 4 * i, to(-1))
            arrive(r_right.at[i], rs_recv.at[5 + 4 * i])
            r = rows(1)
            part[r, RIGHT] = (part[r, RIGHT].astype(F32) + r_right[i].astype(F32)).astype(BF)
            push_sum(part.at[r], r_b.at[i], 7 + 4 * i, to(1))

        def last():
            arrive(r_a.at[i], rs_recv.at[6 + 4 * i])
            arrive(r_b.at[i], rs_recv.at[7 + 4 * i])
            r = rows(0)
            return part[r, :].astype(F32) + r_a[i].astype(F32) + r_b[i].astype(F32)

        return first, middle, last

    rings = []
    for i, dz in enumerate(ORDER):
        arrive(sib_in.at[i], rs_recv.at[i])
        rows = line(c, dz)
        part[rows, :] = (part[rows, :].astype(F32) + sib_in[i].astype(F32)).astype(BF)
        rings.append(ring(i, lambda d, dz=dz: block(c, dz, d), lambda s: dev(g, 0, s, c)))
        rings[i][0]()

    def slope(t):
        cols = pl.ds(t * CH, CH)
        h = hidden[:, cols]
        sg = jax.nn.sigmoid(h)
        gz = scale * (dot(probs[...], table[:, cols]) + pos_weight * pos_rows[:, cols])
        gh[:, cols] = (gz * (sg * (1.0 + h * (1.0 - sg)))).astype(BF)

    def user(t):
        rows = pl.ds(t * CH, CH)
        ug_ref[:, rows] = dot(gh[...], proj[rows, :], 1, 1).astype(BF)

    def gather_back(t):
        cols = pl.ds(t * CH, CH)
        arrive(recv_grads.at[pl.ds(0, 31 * SLOTS), cols], grad_sem.at[1, t])
        back[:, cols] = (scale * dot(pick_ref[...], recv_grads[:, cols], 0, 0)).astype(BF)
        for dy in (1, 3, 2):
            src = pl.ds(pl.multiple_of(lax.rem(y + dy, 4) * ROWS, ROWS), ROWS)
            remote(back.at[src, cols], back_in.at[my_shard, cols], back_sem.at[0, t], back_sem.at[1, t], dev(g, 0, dy, c))
        back_in[my_shard, cols] = back[my_shard, cols]

    slope(0)
    rings[0][1]()
    slope(1)
    rings[1][1]()
    slope(2)
    rings[2][1]()
    slope(3)
    rings[3][1]()
    arrive(weights.at[pl.ds(0, 31)], weight_sem.at[1])
    wide_w = jnp.broadcast_to(weights[...], (32, SLOTS, USERS)).reshape(512, USERS)
    slot_w = jnp.sum(take_ref[...] * wide_w, axis=1, keepdims=True)
    pick_ref[...] = (pick_ref[...].astype(F32) * slot_w).astype(BF)
    gather_back(0)
    lineup = ring(4, lambda d: block(c, d, 0), lambda s: dev(g, s, 0, c))

    def settle(i):
        part[block(c, ORDER[i], 0), :] = rings[i][2]().astype(BF)

    settle(0)
    lineup[0]()
    user(0)
    settle(1)
    settle(2)
    gather_back(1)
    lineup[1]()
    user(1)
    gather_back(2)
    mine = rings[3][2]()
    part[block(c, 0, 0), :] = mine.astype(BF)
    share = lineup[2]()
    for gi in range(4):
        rows8 = share[8 * gi:8 * gi + 8, :]
        xs[4 + gi] = jnp.concatenate([rows8[:, :HALF], rows8[:, HALF:]], axis=0).astype(BF)
    for i in (1, 2, 3):
        gx, to = xpeer(i)
        late.append(remote(xs.at[4 + gx], xr.at[4 + g], x_sem.at[2], x_sem.at[3], to))
    xr[4 + g] = xs[4 + g]
    gather_back(3)
    user(2)
    user(3)
    arrive(xr.at[pl.ds(4, 3)], x_sem.at[3])
    lines = []
    for gi in range(4):
        v = xr[4 + gi].astype(F32)
        lines.append(jnp.concatenate([v[:8], v[8:]], axis=1))
    returned = jnp.concatenate(lines, axis=0).astype(BF)
    for t in range(NC):
        cols = pl.ds(t * CH, CH)
        arrive(back_in.at[pl.ds(0, 192), cols], back_sem.at[1, t])
        acc = dot(pick, returned[:, t * CH:(t + 1) * CH], 0, 0)
        for q in range(4):
            acc = acc + back_in[pl.ds(q * ROWS, ROWS), cols].astype(F32)
        ig_ref[:, cols] = acc

    arrive(xs.at[pl.ds(0, 3)], x_sem.at[0])
    arrive(xs.at[pl.ds(4, 3)], x_sem.at[2])
    arrive(ids.at[pl.ds(0, 31)], ids_sem.at[0])
    arrive(weights.at[pl.ds(0, 31)], weight_sem.at[0])
    for t in range(NC):
        cols = pl.ds(t * CH, CH)
        arrive(shards.at[pl.ds(0, 192), cols], shard_sem.at[0, t])
        arrive(send_slots.at[pl.ds(0, 31 * SLOTS), cols], slot_sem.at[0, t])
        arrive(send_grads.at[pl.ds(0, 31 * SLOTS), cols], grad_sem.at[0, t])
        arrive(back.at[pl.ds(0, 192), cols], back_sem.at[0, t])
    for cp in late[3:-3]:
        cp.wait_send()


def store(ug, ig, ug_out, ig_out, sem):
    copies = [pltpu.make_async_copy(ug, ug_out, sem.at[0]), pltpu.make_async_copy(ig, ig_out, sem.at[1])]
    for cp in copies:
        cp.start()
    for cp in copies:
        cp.wait()


def on_device(user_rows, projection, item_table, positive, negatives):
    vm = pl.BlockSpec(memory_space=pltpu.VMEM)
    hbm = pl.BlockSpec(memory_space=pl.ANY)
    dma = pltpu.SemaphoreType.DMA
    v = pltpu.VMEM
    shapes = (jax.ShapeDtypeStruct((USERS, W), BF), jax.ShapeDtypeStruct((ROWS, W), F32))
    user_grad, item_grad = pl.pallas_call(
        kernel,
        out_shape=shapes,
        in_specs=[hbm] * 5,
        out_specs=(vm, vm),
        scratch_shapes=[
            v((ROWS, W), BF), v((4, 8), I32),
            v((USERS, W), BF), v((W, W), BF), v((USERS, W), F32), v((USERS, W), BF), v((USERS, W), BF),
            v((USERS, 1024), BF), v((USERS, 1024), F32), v((USERS, W), F32),
            v((256, W), BF), v((1024, W), BF), v((32, 1, USERS), I32), v((512, 256), BF),
            v((USERS, 512), BF), v((512, USERS), BF),
            v((512, W), BF), v((512, W), BF), v((512, W), BF), v((512, W), BF),
            v((512, USERS), F32), v((1, USERS), F32), v((32, 1, USERS), F32),
            v((256, W), BF), v((256, W), BF), v((8, 16, HALF), BF), v((8, 16, HALF), BF),
            v((1024, W), BF), v((4, 128, W), BF),
            v((5, 32, HALF), BF), v((5, 32, HALF), BF), v((5, 32, W), BF), v((5, 32, W), BF),
            dma((8,)), dma((2,)), dma((2,)), dma((2, NC)), dma((2, NC)), dma((2, NC)), dma((2, NC)), dma((4,)),
            dma((40,)), dma((32,)), dma((32,)), dma((32,)), dma((24,)), dma((24,)),
        ],
        compiler_params=pltpu.CompilerParams(collective_id=0, has_side_effects=True, vmem_limit_bytes=56 << 20),
        cost_estimate=pl.CostEstimate(flops=5 * 10**9, bytes_accessed=12 * 2**20, transcendentals=10**6),
    )(user_rows, projection, item_table, positive.reshape(1, USERS), negatives)
    return pl.pallas_call(
        store,
        out_shape=shapes,
        in_specs=[vm, vm],
        out_specs=(hbm, hbm),
        scratch_shapes=[dma((2,))],
    )(user_grad, item_grad)


def solution(mesh):
    placed = (
        P(("grp", "mem"), None),
        P(),
        P(("grp", "mem"), None),
        P(("grp", "mem")),
        P(None, ("grp", "mem")),
    )
    return jax.shard_map(
        on_device,
        mesh=mesh,
        in_specs=placed,
        out_specs=(P(("grp", "mem"), None), P(("grp", "mem"), None)),
        check_vma=False,
    )
```

```python
import functools
import math

import jax
import jax.numpy as jnp
from jax import lax
from jax.experimental import pallas as pl
from jax.experimental.pallas import tpu as pltpu
from jax.sharding import PartitionSpec as P

MESH = pl.DeviceIdType.MESH
BF, F32, I32 = jnp.bfloat16, jnp.float32, jnp.int32
W = 2048
HALF = W // 2
CH = 512
NC = W // CH
EARLY = 4
ROWS = 64
USERS = 128
SLOTS = 16
RING = (0, 1, -1, 2)
PLACE = {0: 0, 1: 1, -1: 2, 2: 3}
FULL, LEFT, RIGHT = pl.ds(0, W), pl.ds(0, HALF), pl.ds(HALF, HALF)


def fold(v):
    return {-3: 1, -2: 2, 3: -1}.get(v, v)


def dot(a, b, ca=1, cb=0):
    return lax.dot_general(a, b, (((ca,), (cb,)), ((), ())), preferred_element_type=F32)


def kernel(
    user_hbm, proj_hbm, tab_hbm, pos_hbm, neg_hbm, ug_ref, ig_ref,
    tab, neg_ids, users, proj, hidden, z_ref, gh, probs, logits, pos_rows,
    shards, table, ids, pick_ref, slot_of, slot_to, send_slots, recv_slots, send_grads, recv_grads,
    take_ref, weight_out, weights, back, back_in, xs, xr, part, sib_in, r_left, r_right, r_a, r_b,
    load_sem, ids_sem, weight_sem, shard_sem, slot_sem, grad_sem, back_sem, x_sem,
    ag_send, ag_recv, sib_send, sib_recv, rs_send, rs_recv,
):
    scale = 4.0 / math.sqrt(W)
    g, m = lax.axis_index("grp"), lax.axis_index("mem")
    c, y, zz = lax.rem(m, 2), lax.rem(m // 2, 4), m // 8
    me = (g * 4 + zz) * 2 + c

    def dev(gx, dz, dy, cc):
        return (gx, (lax.rem(zz + dz + 4, 4) * 4 + lax.rem(y + dy + 4, 4)) * 2 + cc)

    def mate(i):
        p = i // 2
        ux, uz, uc = lax.rem(g + p // 4 + p, 4), lax.rem(zz + p, 4), lax.rem(c + i, 2)
        return (ux * 4 + uz) * 2 + uc, (ux, (uz * 4 + y) * 2 + uc)

    def xpeer(i):
        gx = lax.rem(g + i, 4)
        return gx, (gx, m)

    sib = dev(g, 0, 0, 1 - c)
    late = []

    def remote(src, dst, s_sem, r_sem, to):
        cp = pltpu.make_async_remote_copy(
            src_ref=src, dst_ref=dst, send_sem=s_sem, recv_sem=r_sem, device_id=to, device_id_type=MESH
        )
        cp.start()
        return cp

    def arrive(ref, sem):
        pltpu.make_async_copy(ref, ref, sem).wait()

    barrier = pltpu.get_barrier_semaphore()

    def greet(i, carry):
        pl.semaphore_signal(barrier, inc=1, device_id=mate(i)[1], device_id_type=MESH)
        return carry

    lax.fori_loop(1, 32, greet, 0)
    for dy in (1, 2, 3):
        pl.semaphore_signal(barrier, inc=1, device_id=dev(g, 0, dy, c), device_id_type=MESH)

    first_loads = [
        pltpu.make_async_copy(tab_hbm, tab, load_sem.at[5]),
        pltpu.make_async_copy(neg_hbm, neg_ids, load_sem.at[6]),
        pltpu.make_async_copy(pos_hbm, ids.at[me], load_sem.at[7]),
    ]
    for cp in first_loads:
        cp.start()
    loads = [pltpu.make_async_copy(user_hbm, users, load_sem.at[0])]
    for t in range(NC):
        cols = pl.ds(t * CH, CH)
        loads.append(pltpu.make_async_copy(proj_hbm.at[:, cols], proj.at[:, cols], load_sem.at[1 + t]))
    for cp in loads:
        cp.start()

    for cp in first_loads:
        cp.wait()
    pos_lane = ids.at[me]

    diagonal = lax.broadcasted_iota(I32, (8, 8), 0) == lax.broadcasted_iota(I32, (8, 8), 1)
    columns = []
    for gi in range(4):
        wide_ids = jnp.broadcast_to(neg_ids[gi:gi + 1, :], (8, 8)).astype(F32)
        columns.append(jnp.sum(jnp.where(diagonal, wide_ids, 0.0), axis=1, keepdims=True))
    neg_col = jnp.concatenate(columns, axis=0).astype(I32) - (g * 32 + m) * ROWS
    pick = (neg_col == lax.broadcasted_iota(I32, (32, ROWS), 1)).astype(BF)
    picked = dot(pick, tab[...])
    for gi in range(4):
        rows8 = picked[8 * gi:8 * gi + 8, :]
        xs[gi] = jnp.concatenate([rows8[:, :HALF], rows8[:, HALF:]], axis=0).astype(BF)
    my_shard = pl.ds(pl.multiple_of(y * ROWS, ROWS), ROWS)
    for t in range(NC):
        shards[t, my_shard, :] = tab[:, t * CH:(t + 1) * CH]
    pl.semaphore_wait(barrier, 34)

    for i in (1, 2, 3):
        gx, to = xpeer(i)
        late.append(remote(xs.at[gx], xr.at[g], x_sem.at[0], x_sem.at[1], to))
    xr[g] = xs[g]

    def send_ids(i, carry):
        remote(pos_lane, ids.at[me], ids_sem.at[0], ids_sem.at[1], mate(i)[1])
        return carry

    lax.fori_loop(1, 32, send_ids, 0)
    def send_shards(t):
        cols = pl.ds(t * CH, CH)
        for dy in (1, 3, 2):
            remote(tab.at[:, cols], shards.at[t, my_shard], shard_sem.at[0, t], shard_sem.at[1, t], dev(g, 0, dy, c))

    send_shards(0)

    def block(cc, dz, dy):
        at = ((cc * 4 + lax.rem(zz + dz + 4, 4)) * 4 + lax.rem(y + dy + 4, 4)) * 32
        return pl.ds(pl.multiple_of(at, 32), 32)

    def sem_at(f, s, p):
        return (PLACE[f] * 4 + PLACE[s]) * 2 + p

    count = [0]

    def push(f, s, cols, along_z, sgn, p):
        nf, ns = (fold(f - sgn), s) if along_z else (f, fold(s - sgn))
        ref = table.at[block(c, f, s), cols]
        to = dev(g, sgn, 0, c) if along_z else dev(g, 0, sgn, c)
        late.append(remote(ref, ref, ag_send.at[count[0]], ag_recv.at[sem_at(nf, ns, p)], to))
        count[0] += 1

    across = []

    def over(f, s, cols, p):
        ref = table.at[block(c, f, s), cols]
        k = sem_at(f, s, p)
        late.append(remote(ref, ref, sib_send.at[k], sib_recv.at[k], sib))
        across.append((f, s, cols, p))

    def here(f, s, cols, p):
        arrive(table.at[block(c, f, s), cols], ag_recv.at[sem_at(f, s, p)])

    def second(f, cols, p):
        push(f, 0, cols, False, 1, p)
        push(f, 0, cols, False, -1, p)
        over(f, 0, cols, p)

    def relay(f, parts):
        for cols, p in parts:
            for s in (-1, 1):
                here(f, s, cols, p)
                over(f, s, cols, p)
        push(f, -1, LEFT, False, 1, 0)
        push(f, 1, RIGHT, False, -1, 1)

    arrive(xr.at[pl.ds(0, 3)], x_sem.at[1])
    lines = []
    for gi in range(4):
        v = xr[gi].astype(F32)
        lines.append(jnp.concatenate([v[:8], v[8:]], axis=1))
    table[block(c, 0, 0), :] = jnp.concatenate(lines, axis=0).astype(BF)
    push(0, 0, FULL, True, 1, 0)
    push(0, 0, FULL, True, -1, 0)
    second(0, FULL, 0)
    send_shards(1)

    lane = lax.broadcasted_iota(I32, (USERS, USERS), 1)
    sub = lax.broadcasted_iota(I32, (USERS, USERS), 0)
    own_l = pos_lane[...] >> 6
    own_c = jnp.sum(jnp.where(lane == sub, own_l.astype(F32), 0.0), axis=1, keepdims=True).astype(I32)
    same = own_c == own_l
    rank_c = jnp.sum((same & (lane < sub)).astype(F32), axis=1, keepdims=True).astype(I32)
    rank_l = jnp.sum((same & (sub < lane)).astype(F32), axis=0, keepdims=True).astype(I32)

    def slot(o, rank):
        relay_of = ((o >> 5) * 4 + ((o >> 3) & 3)) * 2 + (o & 1)
        return relay_of * SLOTS + ((o >> 1) & 3) * 4 + rank

    slot_of[...] = (slot(own_c, rank_c) == lax.broadcasted_iota(I32, (USERS, 512), 1)).astype(BF)
    slot_to[...] = (slot(own_l, rank_l) == lax.broadcasted_iota(I32, (512, USERS), 0)).astype(BF)

    arrive(ids.at[pl.ds(0, 31)], ids_sem.at[1])
    wide = jnp.broadcast_to(ids[...], (32, SLOTS, USERS)).reshape(512, USERS)
    s_iota = lax.broadcasted_iota(I32, (512, USERS), 0) & (SLOTS - 1)
    owner_q = g * 32 + (zz * 4 + (s_iota >> 2)) * 2 + c
    hit = (wide >> 6) == owner_q
    before = dot(hit.astype(BF), (sub < lane).astype(BF))
    take = hit & (before == (s_iota & 3).astype(F32))
    take_ref[...] = take.astype(F32)
    found = jnp.sum(jnp.where(take, (wide & 63) + 1, 0).astype(F32), axis=1, keepdims=True).astype(I32)
    q_col = (lax.broadcasted_iota(I32, (512, 1), 0) & (SLOTS - 1)) >> 2
    target = jnp.where(found > 0, q_col * ROWS + found - 1, -1)
    pick_ref[...] = (target == lax.broadcasted_iota(I32, (512, 256), 1)).astype(BF)

    def my_slots(u):
        return pl.ds(pl.multiple_of(u * SLOTS, SLOTS), SLOTS)

    def gather(t):
        cols = pl.ds(t * CH, CH)
        arrive(shards.at[t, pl.ds(0, 192)], shard_sem.at[1, t])
        send_slots[t] = dot(pick_ref[...], shards[t]).astype(BF)

        def out(i, carry):
            u, to = mate(i)
            remote(send_slots.at[t, my_slots(u)], recv_slots.at[t, my_slots(me)], slot_sem.at[0, t], slot_sem.at[1, t], to)
            return carry

        lax.fori_loop(1, 32, out, 0)
        recv_slots[t, my_slots(me)] = send_slots[t, my_slots(me)]

    def project(t):
        cols = pl.ds(t * CH, CH)
        loads[1 + t].wait()
        h = dot(users[...], proj[:, cols])
        hidden[:, cols] = h
        z_ref[:, cols] = (h * jax.nn.sigmoid(h)).astype(BF)

    def send_z(t):
        cols = pl.ds(t * CH, CH)
        send_grads[t] = dot(slot_to[...], z_ref[:, cols]).astype(BF)

        def out(i, carry):
            u, to = mate(i)
            remote(send_grads.at[t, my_slots(u)], recv_grads.at[t, my_slots(me)], grad_sem.at[0, t], grad_sem.at[1, t], to)
            return carry

        lax.fori_loop(1, 32, out, 0)
        recv_grads[t, my_slots(me)] = send_grads[t, my_slots(me)]

    loads[0].wait()
    for t in range(NC):
        project(t)
    here(-1, 0, FULL, 0)
    push(-1, 0, LEFT, True, 1, 0)
    here(1, 0, FULL, 0)
    push(1, 0, RIGHT, True, -1, 1)
    second(-1, FULL, 0)
    second(1, FULL, 0)
    send_shards(2)
    send_shards(3)
    gather(0)
    relay(0, [(FULL, 0)])
    gather(1)
    here(2, 0, LEFT, 0)
    second(2, LEFT, 0)
    here(2, 0, RIGHT, 1)
    second(2, RIGHT, 1)
    relay(-1, [(FULL, 0)])
    gather(2)
    relay(1, [(FULL, 0)])
    relay(2, [(LEFT, 0), (RIGHT, 1)])
    gather(3)
    for t in range(EARLY):
        send_z(t)
    for f in RING:
        here(f, 2, LEFT, 0)
        over(f, 2, LEFT, 0)
        here(f, 2, RIGHT, 1)
        over(f, 2, RIGHT, 1)

    def log_rows(cc):
        for t in range(2):
            rows = pl.ds(pl.multiple_of(cc * 512 + t * 256, 256), 256)
            logits[:, rows] = scale * dot(z_ref[...], table[rows, :], 1, 1)

    log_rows(c)
    for f, s, cols, p in across:
        arrive(table.at[block(1 - c, f, s), cols], sib_recv.at[sem_at(f, s, p)])
    log_rows(1 - c)
    pos_logit = jnp.zeros((USERS, 1), F32)
    for t in range(NC):
        cols = pl.ds(t * CH, CH)
        arrive(recv_slots.at[t, pl.ds(0, 31 * SLOTS)], slot_sem.at[1, t])
        pr = dot(slot_of[...], recv_slots[t])
        pos_rows[:, cols] = pr
        pos_logit = pos_logit + jnp.sum(z_ref[:, cols].astype(F32) * pr, axis=1, keepdims=True)
    pos_logit = scale * pos_logit
    lg = logits[...]
    top = jnp.maximum(pos_logit, jnp.max(lg, axis=1, keepdims=True))
    total = jnp.exp(pos_logit - top) + jnp.sum(jnp.exp(lg - top), axis=1, keepdims=True)
    log_total = top + jnp.log(total)
    probs[...] = jnp.exp(lg - log_total).astype(BF)
    pos_weight = jnp.exp(pos_logit - log_total) - 1.0

    weight_out[...] = jnp.sum(jnp.where(lane == sub, pos_weight, 0.0), axis=0, keepdims=True)
    weights[me] = weight_out[...]

    def send_weights(i, carry):
        remote(weight_out, weights.at[me], weight_sem.at[0], weight_sem.at[1], mate(i)[1])
        return carry

    lax.fori_loop(1, 32, send_weights, 0)
    for t in range(EARLY, NC):
        send_z(t)

    def line(cc, dz):
        return pl.ds(pl.multiple_of((cc * 4 + lax.rem(zz + dz + 4, 4)) * 128, 128), 128)

    ORDER = (2, 1, -1, 0)
    for i, dz in enumerate(ORDER):
        for cc in (1 - c, c):
            rows = line(cc, dz)
            pt = probs[:, rows]
            for t in range(NC):
                cols = pl.ds(t * CH, CH)
                part[rows, cols] = dot(pt, z_ref[:, cols], 0, 0).astype(BF)
        late.append(remote(part.at[line(1 - c, dz)], sib_in.at[i], rs_send.at[i], rs_recv.at[i], sib))

    rs_count = [4]

    def push_sum(src, dst, k, to):
        late.append(remote(src, dst, rs_send.at[rs_count[0]], rs_recv.at[k], to))
        rs_count[0] += 1

    def ring(i, rows, to):
        def first():
            push_sum(part.at[rows(2), LEFT], r_left.at[i], 4 + 4 * i, to(-1))
            push_sum(part.at[rows(2), RIGHT], r_right.at[i], 5 + 4 * i, to(1))

        def middle():
            arrive(r_left.at[i], rs_recv.at[4 + 4 * i])
            r = rows(-1)
            part[r, LEFT] = (part[r, LEFT].astype(F32) + r_left[i].astype(F32)).astype(BF)
            push_sum(part.at[r], r_a.at[i], 6 + 4 * i, to(-1))
            arrive(r_right.at[i], rs_recv.at[5 + 4 * i])
            r = rows(1)
            part[r, RIGHT] = (part[r, RIGHT].astype(F32) + r_right[i].astype(F32)).astype(BF)
            push_sum(part.at[r], r_b.at[i], 7 + 4 * i, to(1))

        def last():
            arrive(r_a.at[i], rs_recv.at[6 + 4 * i])
            arrive(r_b.at[i], rs_recv.at[7 + 4 * i])
            r = rows(0)
            return part[r, :].astype(F32) + r_a[i].astype(F32) + r_b[i].astype(F32)

        return first, middle, last

    rings = []
    for i, dz in enumerate(ORDER):
        arrive(sib_in.at[i], rs_recv.at[i])
        rows = line(c, dz)
        part[rows, :] = (part[rows, :].astype(F32) + sib_in[i].astype(F32)).astype(BF)
        rings.append(ring(i, lambda d, dz=dz: block(c, dz, d), lambda s: dev(g, 0, s, c)))
        rings[i][0]()

    def slope(t):
        cols = pl.ds(t * CH, CH)
        h = hidden[:, cols]
        sg = jax.nn.sigmoid(h)
        gz = scale * (dot(probs[...], table[:, cols]) + pos_weight * pos_rows[:, cols])
        gh[:, cols] = (gz * (sg * (1.0 + h * (1.0 - sg)))).astype(BF)

    def user(t):
        rows = pl.ds(t * CH, CH)
        ug_ref[:, rows] = dot(gh[...], proj[rows, :], 1, 1).astype(BF)

    def gather_back(t):
        cols = pl.ds(t * CH, CH)
        arrive(recv_grads.at[t, pl.ds(0, 31 * SLOTS)], grad_sem.at[1, t])
        back[t] = dot(pick_ref[...], recv_grads[t], 0, 0).astype(BF)
        for dy in (1, 3, 2):
            src = pl.ds(pl.multiple_of(lax.rem(y + dy, 4) * ROWS, ROWS), ROWS)
            remote(back.at[t, src], back_in.at[t, my_shard], back_sem.at[0, t], back_sem.at[1, t], dev(g, 0, dy, c))
        back_in[t, my_shard] = back[t, my_shard]

    slope(0)
    rings[0][1]()
    rings[1][1]()
    slope(1)
    rings[2][1]()
    rings[3][1]()
    slope(2)
    slope(3)
    arrive(weights.at[pl.ds(0, 31)], weight_sem.at[1])
    wide_w = jnp.broadcast_to(weights[...], (32, SLOTS, USERS)).reshape(512, USERS)
    slot_w = jnp.sum(take_ref[...] * wide_w, axis=1, keepdims=True)
    pick_ref[...] = (pick_ref[...].astype(F32) * slot_w).astype(BF)
    gather_back(0)
    lineup = ring(4, lambda d: block(c, d, 0), lambda s: dev(g, s, 0, c))

    def settle(i):
        part[block(c, ORDER[i], 0), :] = rings[i][2]().astype(BF)

    settle(0)
    lineup[0]()
    user(0)
    settle(1)
    settle(2)
    gather_back(1)
    lineup[1]()
    user(1)
    gather_back(2)
    mine = rings[3][2]()
    part[block(c, 0, 0), :] = mine.astype(BF)
    share = lineup[2]()
    for gi in range(4):
        rows8 = share[8 * gi:8 * gi + 8, :]
        xs[4 + gi] = jnp.concatenate([rows8[:, :HALF], rows8[:, HALF:]], axis=0).astype(BF)
    for i in (1, 2, 3):
        gx, to = xpeer(i)
        late.append(remote(xs.at[4 + gx], xr.at[4 + g], x_sem.at[2], x_sem.at[3], to))
    xr[4 + g] = xs[4 + g]
    gather_back(3)
    user(2)
    user(3)
    arrive(xr.at[pl.ds(4, 3)], x_sem.at[3])
    lines = []
    for gi in range(4):
        v = xr[4 + gi].astype(F32)
        lines.append(jnp.concatenate([v[:8], v[8:]], axis=1))
    returned = jnp.concatenate(lines, axis=0).astype(BF)
    for t in range(NC):
        cols = pl.ds(t * CH, CH)
        arrive(back_in.at[t, pl.ds(0, 192)], back_sem.at[1, t])
        acc = dot(pick, returned[:, t * CH:(t + 1) * CH], 0, 0)
        for q in range(4):
            acc = acc + back_in[t, pl.ds(q * ROWS, ROWS)].astype(F32)
        ig_ref[:, cols] = scale * acc

    arrive(xs.at[pl.ds(0, 3)], x_sem.at[0])
    arrive(xs.at[pl.ds(4, 3)], x_sem.at[2])
    arrive(ids.at[pl.ds(0, 31)], ids_sem.at[0])
    arrive(weights.at[pl.ds(0, 31)], weight_sem.at[0])
    for t in range(NC):
        cols = pl.ds(t * CH, CH)
        arrive(shards.at[t, pl.ds(0, 192)], shard_sem.at[0, t])
        arrive(send_slots.at[t, pl.ds(0, 31 * SLOTS)], slot_sem.at[0, t])
        arrive(send_grads.at[t, pl.ds(0, 31 * SLOTS)], grad_sem.at[0, t])
        arrive(back.at[t, pl.ds(0, 192)], back_sem.at[0, t])
    for cp in late[3:-3]:
        cp.wait_send()


def store(ug, ig, ug_out, ig_out, sem):
    copies = []
    for src, dst in ((ug, ug_out), (ig, ig_out)):
        n = src.shape[0] // 4
        for k in range(4):
            rows = pl.ds(k * n, n)
            copies.append(pltpu.make_async_copy(src.at[rows], dst.at[rows], sem.at[len(copies)]))
    for cp in copies:
        cp.start()
    for cp in copies:
        cp.wait()


def on_device(user_rows, projection, item_table, positive, negatives):
    vm = pl.BlockSpec(memory_space=pltpu.VMEM)
    hbm = pl.BlockSpec(memory_space=pl.ANY)
    dma = pltpu.SemaphoreType.DMA
    v = pltpu.VMEM
    shapes = (jax.ShapeDtypeStruct((USERS, W), BF), jax.ShapeDtypeStruct((ROWS, W), F32))
    user_grad, item_grad = pl.pallas_call(
        kernel,
        out_shape=shapes,
        in_specs=[hbm] * 5,
        out_specs=(vm, vm),
        scratch_shapes=[
            v((ROWS, W), BF), v((4, 8), I32),
            v((USERS, W), BF), v((W, W), BF), v((USERS, W), F32), v((USERS, W), BF), v((USERS, W), BF),
            v((USERS, 1024), BF), v((USERS, 1024), F32), v((USERS, W), F32),
            v((NC, 256, CH), BF), v((1024, W), BF), v((32, 1, USERS), I32), v((512, 256), BF),
            v((USERS, 512), BF), v((512, USERS), BF),
            v((NC, 512, CH), BF), v((NC, 512, CH), BF), v((NC, 512, CH), BF), v((NC, 512, CH), BF),
            v((512, USERS), F32), v((1, USERS), F32), v((32, 1, USERS), F32),
            v((NC, 256, CH), BF), v((NC, 256, CH), BF), v((8, 16, HALF), BF), v((8, 16, HALF), BF),
            v((1024, W), BF), v((4, 128, W), BF),
            v((5, 32, HALF), BF), v((5, 32, HALF), BF), v((5, 32, W), BF), v((5, 32, W), BF),
            dma((8,)), dma((2,)), dma((2,)), dma((2, NC)), dma((2, NC)), dma((2, NC)), dma((2, NC)), dma((4,)),
            dma((40,)), dma((32,)), dma((32,)), dma((32,)), dma((24,)), dma((24,)),
        ],
        compiler_params=pltpu.CompilerParams(collective_id=0, has_side_effects=True, vmem_limit_bytes=56 << 20),
        cost_estimate=pl.CostEstimate(flops=5 * 10**9, bytes_accessed=12 * 2**20, transcendentals=10**6),
    )(user_rows, projection, item_table, positive.reshape(1, USERS), negatives)
    return pl.pallas_call(
        store,
        out_shape=shapes,
        in_specs=[vm, vm],
        out_specs=(hbm, hbm),
        scratch_shapes=[dma((8,))],
    )(user_grad, item_grad)


def solution(mesh):
    placed = (
        P(("grp", "mem"), None),
        P(),
        P(("grp", "mem"), None),
        P(("grp", "mem")),
        P(None, ("grp", "mem")),
    )
    return jax.shard_map(
        on_device,
        mesh=mesh,
        in_specs=placed,
        out_specs=(P(("grp", "mem"), None), P(("grp", "mem"), None)),
        check_vma=False,
    )
```

```python
import functools
import math

import jax
import jax.numpy as jnp
from jax import lax
from jax.experimental import pallas as pl
from jax.experimental.pallas import tpu as pltpu
from jax.sharding import PartitionSpec as P

MESH = pl.DeviceIdType.MESH
BF, F32, I32 = jnp.bfloat16, jnp.float32, jnp.int32
W = 2048
HALF = W // 2
CH = 512
NC = W // CH
EARLY = 4
ROWS = 64
USERS = 128
SLOTS = 16
RING = (0, 1, -1, 2)
PLACE = {0: 0, 1: 1, -1: 2, 2: 3}
FULL, LEFT, RIGHT = pl.ds(0, W), pl.ds(0, HALF), pl.ds(HALF, HALF)


def fold(v):
    return {-3: 1, -2: 2, 3: -1}.get(v, v)


def dot(a, b, ca=1, cb=0):
    return lax.dot_general(a, b, (((ca,), (cb,)), ((), ())), preferred_element_type=F32)


def kernel(
    user_hbm, proj_hbm, tab_hbm, pos_hbm, neg_hbm, ug_ref, ig_ref,
    tab, neg_ids, users, proj, hidden, z_ref, gh, probs, logits, pos_rows,
    shards, table, ids, pick_ref, slot_of, slot_to, send_slots, recv_slots, send_grads, recv_grads,
    take_ref, weight_out, weights, back, back_in, xs, xr, part, sib_in, r_left, r_right, r_a, r_b,
    load_sem, ids_sem, weight_sem, shard_sem, slot_sem, grad_sem, back_sem, x_sem,
    ag_send, ag_recv, sib_send, sib_recv, rs_send, rs_recv,
):
    scale = 4.0 / math.sqrt(W)
    g, m = lax.axis_index("grp"), lax.axis_index("mem")
    c, y, zz = lax.rem(m, 2), lax.rem(m // 2, 4), m // 8
    me = (g * 4 + zz) * 2 + c

    def dev(gx, dz, dy, cc):
        return (gx, (lax.rem(zz + dz + 4, 4) * 4 + lax.rem(y + dy + 4, 4)) * 2 + cc)

    def mate(i):
        p = i // 2
        ux, uz, uc = lax.rem(g + p // 4 + p, 4), lax.rem(zz + p, 4), lax.rem(c + i, 2)
        return (ux * 4 + uz) * 2 + uc, (ux, (uz * 4 + y) * 2 + uc)

    def xpeer(i):
        gx = lax.rem(g + i, 4)
        return gx, (gx, m)

    sib = dev(g, 0, 0, 1 - c)
    late = []

    def remote(src, dst, s_sem, r_sem, to):
        cp = pltpu.make_async_remote_copy(
            src_ref=src, dst_ref=dst, send_sem=s_sem, recv_sem=r_sem, device_id=to, device_id_type=MESH
        )
        cp.start()
        return cp

    def arrive(ref, sem):
        pltpu.make_async_copy(ref, ref, sem).wait()

    barrier = pltpu.get_barrier_semaphore()

    def greet(i, carry):
        pl.semaphore_signal(barrier, inc=1, device_id=mate(i)[1], device_id_type=MESH)
        return carry

    lax.fori_loop(1, 32, greet, 0)
    for dy in (1, 2, 3):
        pl.semaphore_signal(barrier, inc=1, device_id=dev(g, 0, dy, c), device_id_type=MESH)

    first_loads = [
        pltpu.make_async_copy(tab_hbm, tab, load_sem.at[5]),
        pltpu.make_async_copy(neg_hbm, neg_ids, load_sem.at[6]),
        pltpu.make_async_copy(pos_hbm, ids.at[me], load_sem.at[7]),
    ]
    for cp in first_loads:
        cp.start()
    loads = [pltpu.make_async_copy(user_hbm, users, load_sem.at[0])]
    for t in range(NC):
        cols = pl.ds(t * CH, CH)
        loads.append(pltpu.make_async_copy(proj_hbm.at[:, cols], proj.at[:, cols], load_sem.at[1 + t]))
    for cp in loads:
        cp.start()

    for cp in first_loads:
        cp.wait()
    pos_lane = ids.at[me]

    diagonal = lax.broadcasted_iota(I32, (8, 8), 0) == lax.broadcasted_iota(I32, (8, 8), 1)
    columns = []
    for gi in range(4):
        wide_ids = jnp.broadcast_to(neg_ids[gi:gi + 1, :], (8, 8)).astype(F32)
        columns.append(jnp.sum(jnp.where(diagonal, wide_ids, 0.0), axis=1, keepdims=True))
    neg_col = jnp.concatenate(columns, axis=0).astype(I32) - (g * 32 + m) * ROWS
    pick = (neg_col == lax.broadcasted_iota(I32, (32, ROWS), 1)).astype(BF)
    picked = dot(pick, tab[...])
    for gi in range(4):
        rows8 = picked[8 * gi:8 * gi + 8, :]
        xs[gi] = jnp.concatenate([rows8[:, :HALF], rows8[:, HALF:]], axis=0).astype(BF)
    my_shard = pl.ds(pl.multiple_of(y * ROWS, ROWS), ROWS)
    for t in range(NC):
        shards[t, my_shard, :] = tab[:, t * CH:(t + 1) * CH]
    pl.semaphore_wait(barrier, 34)

    for i in (1, 2, 3):
        gx, to = xpeer(i)
        late.append(remote(xs.at[gx], xr.at[g], x_sem.at[0], x_sem.at[1], to))
    xr[g] = xs[g]

    def send_ids(i, carry):
        remote(pos_lane, ids.at[me], ids_sem.at[0], ids_sem.at[1], mate(i)[1])
        return carry

    lax.fori_loop(1, 32, send_ids, 0)
    def send_shards(t):
        cols = pl.ds(t * CH, CH)
        for dy in (1, 3, 2):
            remote(tab.at[:, cols], shards.at[t, my_shard], shard_sem.at[0, t], shard_sem.at[1, t], dev(g, 0, dy, c))

    send_shards(0)

    def block(cc, dz, dy):
        at = ((cc * 4 + lax.rem(zz + dz + 4, 4)) * 4 + lax.rem(y + dy + 4, 4)) * 32
        return pl.ds(pl.multiple_of(at, 32), 32)

    def sem_at(f, s, p):
        return (PLACE[f] * 4 + PLACE[s]) * 2 + p

    count = [0]

    def push(f, s, cols, along_z, sgn, p):
        nf, ns = (fold(f - sgn), s) if along_z else (f, fold(s - sgn))
        ref = table.at[block(c, f, s), cols]
        to = dev(g, sgn, 0, c) if along_z else dev(g, 0, sgn, c)
        late.append(remote(ref, ref, ag_send.at[count[0]], ag_recv.at[sem_at(nf, ns, p)], to))
        count[0] += 1

    across = []

    def over(f, s, cols, p):
        ref = table.at[block(c, f, s), cols]
        k = sem_at(f, s, p)
        late.append(remote(ref, ref, sib_send.at[k], sib_recv.at[k], sib))
        across.append((f, s, cols, p))

    def here(f, s, cols, p):
        arrive(table.at[block(c, f, s), cols], ag_recv.at[sem_at(f, s, p)])

    def second(f, cols, p):
        push(f, 0, cols, False, 1, p)
        push(f, 0, cols, False, -1, p)
        over(f, 0, cols, p)

    def relay(f, parts):
        for cols, p in parts:
            for s in (-1, 1):
                here(f, s, cols, p)
                over(f, s, cols, p)
        push(f, -1, LEFT, False, 1, 0)
        push(f, 1, RIGHT, False, -1, 1)

    arrive(xr.at[pl.ds(0, 3)], x_sem.at[1])
    lines = []
    for gi in range(4):
        v = xr[gi].astype(F32)
        lines.append(jnp.concatenate([v[:8], v[8:]], axis=1))
    table[block(c, 0, 0), :] = jnp.concatenate(lines, axis=0).astype(BF)
    push(0, 0, FULL, True, 1, 0)
    push(0, 0, FULL, True, -1, 0)
    second(0, FULL, 0)
    send_shards(1)

    lane = lax.broadcasted_iota(I32, (USERS, USERS), 1)
    sub = lax.broadcasted_iota(I32, (USERS, USERS), 0)
    own_l = pos_lane[...] >> 6
    own_c = jnp.sum(jnp.where(lane == sub, own_l.astype(F32), 0.0), axis=1, keepdims=True).astype(I32)
    same = own_c == own_l
    rank_c = jnp.sum((same & (lane < sub)).astype(F32), axis=1, keepdims=True).astype(I32)
    rank_l = jnp.sum((same & (sub < lane)).astype(F32), axis=0, keepdims=True).astype(I32)

    def slot(o, rank):
        relay_of = ((o >> 5) * 4 + ((o >> 3) & 3)) * 2 + (o & 1)
        return relay_of * SLOTS + ((o >> 1) & 3) * 4 + rank

    slot_of[...] = (slot(own_c, rank_c) == lax.broadcasted_iota(I32, (USERS, 512), 1)).astype(BF)
    slot_to[...] = (slot(own_l, rank_l) == lax.broadcasted_iota(I32, (512, USERS), 0)).astype(BF)

    arrive(ids.at[pl.ds(0, 31)], ids_sem.at[1])
    wide = jnp.broadcast_to(ids[...], (32, SLOTS, USERS)).reshape(512, USERS)
    s_iota = lax.broadcasted_iota(I32, (512, USERS), 0) & (SLOTS - 1)
    owner_q = g * 32 + (zz * 4 + (s_iota >> 2)) * 2 + c
    hit = (wide >> 6) == owner_q
    before = dot(hit.astype(BF), (sub < lane).astype(BF))
    take = hit & (before == (s_iota & 3).astype(F32))
    take_ref[...] = take.astype(F32)
    found = jnp.sum(jnp.where(take, (wide & 63) + 1, 0).astype(F32), axis=1, keepdims=True).astype(I32)
    q_col = (lax.broadcasted_iota(I32, (512, 1), 0) & (SLOTS - 1)) >> 2
    target = jnp.where(found > 0, q_col * ROWS + found - 1, -1)
    pick_ref[...] = (target == lax.broadcasted_iota(I32, (512, 256), 1)).astype(BF)

    def my_slots(u):
        return pl.ds(pl.multiple_of(u * SLOTS, SLOTS), SLOTS)

    def gather(t):
        cols = pl.ds(t * CH, CH)
        arrive(shards.at[t, pl.ds(0, 192)], shard_sem.at[1, t])
        send_slots[t] = dot(pick_ref[...], shards[t]).astype(BF)

        def out(i, carry):
            u, to = mate(i)
            remote(send_slots.at[t, my_slots(u)], recv_slots.at[t, my_slots(me)], slot_sem.at[0, t], slot_sem.at[1, t], to)
            return carry

        lax.fori_loop(1, 32, out, 0)
        recv_slots[t, my_slots(me)] = send_slots[t, my_slots(me)]

    def project(t):
        cols = pl.ds(t * CH, CH)
        loads[1 + t].wait()
        h = dot(users[...], proj[:, cols])
        hidden[:, cols] = h
        z_ref[:, cols] = (h * jax.nn.sigmoid(h)).astype(BF)

    def send_z(t):
        cols = pl.ds(t * CH, CH)
        send_grads[t] = dot(slot_to[...], z_ref[:, cols]).astype(BF)

        def out(i, carry):
            u, to = mate(i)
            remote(send_grads.at[t, my_slots(u)], recv_grads.at[t, my_slots(me)], grad_sem.at[0, t], grad_sem.at[1, t], to)
            return carry

        lax.fori_loop(1, 32, out, 0)
        recv_grads[t, my_slots(me)] = send_grads[t, my_slots(me)]

    loads[0].wait()
    for t in range(NC):
        project(t)
    here(-1, 0, FULL, 0)
    push(-1, 0, LEFT, True, 1, 0)
    here(1, 0, FULL, 0)
    push(1, 0, RIGHT, True, -1, 1)
    second(-1, FULL, 0)
    second(1, FULL, 0)
    gather(0)
    send_shards(2)
    relay(0, [(FULL, 0)])
    gather(1)
    send_shards(3)
    here(2, 0, LEFT, 0)
    second(2, LEFT, 0)
    here(2, 0, RIGHT, 1)
    second(2, RIGHT, 1)
    relay(-1, [(FULL, 0)])
    gather(2)
    relay(1, [(FULL, 0)])
    relay(2, [(LEFT, 0), (RIGHT, 1)])
    gather(3)
    for t in range(EARLY):
        send_z(t)
    for f in RING:
        here(f, 2, LEFT, 0)
        over(f, 2, LEFT, 0)
        here(f, 2, RIGHT, 1)
        over(f, 2, RIGHT, 1)

    def log_rows(cc):
        for t in range(2):
            rows = pl.ds(pl.multiple_of(cc * 512 + t * 256, 256), 256)
            logits[:, rows] = scale * dot(z_ref[...], table[rows, :], 1, 1)

    log_rows(c)
    for f, s, cols, p in across:
        arrive(table.at[block(1 - c, f, s), cols], sib_recv.at[sem_at(f, s, p)])
    log_rows(1 - c)
    pos_logit = jnp.zeros((USERS, 1), F32)
    for t in range(NC):
        cols = pl.ds(t * CH, CH)
        arrive(recv_slots.at[t, pl.ds(0, 31 * SLOTS)], slot_sem.at[1, t])
        pr = dot(slot_of[...], recv_slots[t])
        pos_rows[:, cols] = pr
        pos_logit = pos_logit + jnp.sum(z_ref[:, cols].astype(F32) * pr, axis=1, keepdims=True)
    pos_logit = scale * pos_logit
    lg = logits[...]
    top = jnp.maximum(pos_logit, jnp.max(lg, axis=1, keepdims=True))
    total = jnp.exp(pos_logit - top) + jnp.sum(jnp.exp(lg - top), axis=1, keepdims=True)
    log_total = top + jnp.log(total)
    probs[...] = jnp.exp(lg - log_total).astype(BF)
    pos_weight = jnp.exp(pos_logit - log_total) - 1.0

    weight_out[...] = jnp.sum(jnp.where(lane == sub, pos_weight, 0.0), axis=0, keepdims=True)
    weights[me] = weight_out[...]

    def send_weights(i, carry):
        remote(weight_out, weights.at[me], weight_sem.at[0], weight_sem.at[1], mate(i)[1])
        return carry

    lax.fori_loop(1, 32, send_weights, 0)
    for t in range(EARLY, NC):
        send_z(t)

    def line(cc, dz):
        return pl.ds(pl.multiple_of((cc * 4 + lax.rem(zz + dz + 4, 4)) * 128, 128), 128)

    ORDER = (2, 1, -1, 0)
    for i, dz in enumerate(ORDER):
        for cc in (1 - c, c):
            rows = line(cc, dz)
            pt = probs[:, rows]
            for t in range(NC):
                cols = pl.ds(t * CH, CH)
                part[rows, cols] = dot(pt, z_ref[:, cols], 0, 0).astype(BF)
        late.append(remote(part.at[line(1 - c, dz)], sib_in.at[i], rs_send.at[i], rs_recv.at[i], sib))

    rs_count = [4]

    def push_sum(src, dst, k, to):
        late.append(remote(src, dst, rs_send.at[rs_count[0]], rs_recv.at[k], to))
        rs_count[0] += 1

    def ring(i, rows, to):
        def first():
            push_sum(part.at[rows(2), LEFT], r_left.at[i], 4 + 4 * i, to(-1))
            push_sum(part.at[rows(2), RIGHT], r_right.at[i], 5 + 4 * i, to(1))

        def middle():
            arrive(r_left.at[i], rs_recv.at[4 + 4 * i])
            r = rows(-1)
            part[r, LEFT] = (part[r, LEFT].astype(F32) + r_left[i].astype(F32)).astype(BF)
            push_sum(part.at[r], r_a.at[i], 6 + 4 * i, to(-1))
            arrive(r_right.at[i], rs_recv.at[5 + 4 * i])
            r = rows(1)
            part[r, RIGHT] = (part[r, RIGHT].astype(F32) + r_right[i].astype(F32)).astype(BF)
            push_sum(part.at[r], r_b.at[i], 7 + 4 * i, to(1))

        def last():
            arrive(r_a.at[i], rs_recv.at[6 + 4 * i])
            arrive(r_b.at[i], rs_recv.at[7 + 4 * i])
            r = rows(0)
            return part[r, :].astype(F32) + r_a[i].astype(F32) + r_b[i].astype(F32)

        return first, middle, last

    rings = []
    for i, dz in enumerate(ORDER):
        arrive(sib_in.at[i], rs_recv.at[i])
        rows = line(c, dz)
        part[rows, :] = (part[rows, :].astype(F32) + sib_in[i].astype(F32)).astype(BF)
        rings.append(ring(i, lambda d, dz=dz: block(c, dz, d), lambda s: dev(g, 0, s, c)))
        rings[i][0]()

    def slope(t):
        cols = pl.ds(t * CH, CH)
        h = hidden[:, cols]
        sg = jax.nn.sigmoid(h)
        gz = scale * (dot(probs[...], table[:, cols]) + pos_weight * pos_rows[:, cols])
        gh[:, cols] = (gz * (sg * (1.0 + h * (1.0 - sg)))).astype(BF)

    def user(t):
        rows = pl.ds(t * CH, CH)
        ug_ref[:, rows] = dot(gh[...], proj[rows, :], 1, 1).astype(BF)

    def gather_back(t):
        cols = pl.ds(t * CH, CH)
        arrive(recv_grads.at[t, pl.ds(0, 31 * SLOTS)], grad_sem.at[1, t])
        back[t] = dot(pick_ref[...], recv_grads[t], 0, 0).astype(BF)
        for dy in (1, 3, 2):
            src = pl.ds(pl.multiple_of(lax.rem(y + dy, 4) * ROWS, ROWS), ROWS)
            remote(back.at[t, src], back_in.at[t, my_shard], back_sem.at[0, t], back_sem.at[1, t], dev(g, 0, dy, c))
        back_in[t, my_shard] = back[t, my_shard]

    slope(0)
    rings[0][1]()
    rings[1][1]()
    slope(1)
    rings[2][1]()
    rings[3][1]()
    slope(2)
    slope(3)
    arrive(weights.at[pl.ds(0, 31)], weight_sem.at[1])
    wide_w = jnp.broadcast_to(weights[...], (32, SLOTS, USERS)).reshape(512, USERS)
    slot_w = jnp.sum(take_ref[...] * wide_w, axis=1, keepdims=True)
    pick_ref[...] = (pick_ref[...].astype(F32) * slot_w).astype(BF)
    lineup = ring(4, lambda d: block(c, d, 0), lambda s: dev(g, s, 0, c))

    def settle(i):
        part[block(c, ORDER[i], 0), :] = rings[i][2]().astype(BF)

    settle(0)
    lineup[0]()
    gather_back(0)
    user(0)
    settle(1)
    settle(2)
    gather_back(1)
    lineup[1]()
    user(1)
    gather_back(2)
    mine = rings[3][2]()
    part[block(c, 0, 0), :] = mine.astype(BF)
    share = lineup[2]()
    for gi in range(4):
        rows8 = share[8 * gi:8 * gi + 8, :]
        xs[4 + gi] = jnp.concatenate([rows8[:, :HALF], rows8[:, HALF:]], axis=0).astype(BF)
    for i in (1, 2, 3):
        gx, to = xpeer(i)
        late.append(remote(xs.at[4 + gx], xr.at[4 + g], x_sem.at[2], x_sem.at[3], to))
    xr[4 + g] = xs[4 + g]
    gather_back(3)
    user(2)
    user(3)
    arrive(xr.at[pl.ds(4, 3)], x_sem.at[3])
    lines = []
    for gi in range(4):
        v = xr[4 + gi].astype(F32)
        lines.append(jnp.concatenate([v[:8], v[8:]], axis=1))
    returned = jnp.concatenate(lines, axis=0).astype(BF)
    for t in range(NC):
        cols = pl.ds(t * CH, CH)
        arrive(back_in.at[t, pl.ds(0, 192)], back_sem.at[1, t])
        acc = dot(pick, returned[:, t * CH:(t + 1) * CH], 0, 0)
        for q in range(4):
            acc = acc + back_in[t, pl.ds(q * ROWS, ROWS)].astype(F32)
        ig_ref[:, cols] = scale * acc

    arrive(xs.at[pl.ds(0, 3)], x_sem.at[0])
    arrive(xs.at[pl.ds(4, 3)], x_sem.at[2])
    arrive(ids.at[pl.ds(0, 31)], ids_sem.at[0])
    arrive(weights.at[pl.ds(0, 31)], weight_sem.at[0])
    for t in range(NC):
        cols = pl.ds(t * CH, CH)
        arrive(shards.at[t, pl.ds(0, 192)], shard_sem.at[0, t])
        arrive(send_slots.at[t, pl.ds(0, 31 * SLOTS)], slot_sem.at[0, t])
        arrive(send_grads.at[t, pl.ds(0, 31 * SLOTS)], grad_sem.at[0, t])
        arrive(back.at[t, pl.ds(0, 192)], back_sem.at[0, t])
    for cp in late[3:-3]:
        cp.wait_send()


def store(ug, ig, ug_out, ig_out, sem):
    copies = []
    for src, dst in ((ug, ug_out), (ig, ig_out)):
        n = src.shape[0] // 4
        for k in range(4):
            rows = pl.ds(k * n, n)
            copies.append(pltpu.make_async_copy(src.at[rows], dst.at[rows], sem.at[len(copies)]))
    for cp in copies:
        cp.start()
    for cp in copies:
        cp.wait()


def on_device(user_rows, projection, item_table, positive, negatives):
    vm = pl.BlockSpec(memory_space=pltpu.VMEM)
    hbm = pl.BlockSpec(memory_space=pl.ANY)
    dma = pltpu.SemaphoreType.DMA
    v = pltpu.VMEM
    shapes = (jax.ShapeDtypeStruct((USERS, W), BF), jax.ShapeDtypeStruct((ROWS, W), F32))
    user_grad, item_grad = pl.pallas_call(
        kernel,
        out_shape=shapes,
        in_specs=[hbm] * 5,
        out_specs=(vm, vm),
        scratch_shapes=[
            v((ROWS, W), BF), v((4, 8), I32),
            v((USERS, W), BF), v((W, W), BF), v((USERS, W), F32), v((USERS, W), BF), v((USERS, W), BF),
            v((USERS, 1024), BF), v((USERS, 1024), F32), v((USERS, W), F32),
            v((NC, 256, CH), BF), v((1024, W), BF), v((32, 1, USERS), I32), v((512, 256), BF),
            v((USERS, 512), BF), v((512, USERS), BF),
            v((NC, 512, CH), BF), v((NC, 512, CH), BF), v((NC, 512, CH), BF), v((NC, 512, CH), BF),
            v((512, USERS), F32), v((1, USERS), F32), v((32, 1, USERS), F32),
            v((NC, 256, CH), BF), v((NC, 256, CH), BF), v((8, 16, HALF), BF), v((8, 16, HALF), BF),
            v((1024, W), BF), v((4, 128, W), BF),
            v((5, 32, HALF), BF), v((5, 32, HALF), BF), v((5, 32, W), BF), v((5, 32, W), BF),
            dma((8,)), dma((2,)), dma((2,)), dma((2, NC)), dma((2, NC)), dma((2, NC)), dma((2, NC)), dma((4,)),
            dma((40,)), dma((32,)), dma((32,)), dma((32,)), dma((24,)), dma((24,)),
        ],
        compiler_params=pltpu.CompilerParams(collective_id=0, has_side_effects=True, vmem_limit_bytes=56 << 20),
        cost_estimate=pl.CostEstimate(flops=5 * 10**9, bytes_accessed=12 * 2**20, transcendentals=10**6),
    )(user_rows, projection, item_table, positive.reshape(1, USERS), negatives)
    return pl.pallas_call(
        store,
        out_shape=shapes,
        in_specs=[vm, vm],
        out_specs=(hbm, hbm),
        scratch_shapes=[dma((8,))],
    )(user_grad, item_grad)


def solution(mesh):
    placed = (
        P(("grp", "mem"), None),
        P(),
        P(("grp", "mem"), None),
        P(("grp", "mem")),
        P(None, ("grp", "mem")),
    )
    return jax.shard_map(
        on_device,
        mesh=mesh,
        in_specs=placed,
        out_specs=(P(("grp", "mem"), None), P(("grp", "mem"), None)),
        check_vma=False,
    )
```
